128 devices in a mesh: prow: 16 (over z, x), pcol: 8 (over y, core).
Axes of the slice: x: 4, y: 4, z: 4, core: 2. Of those that a mesh axis runs over, the one named last changes fastest.
Arguments:
- panel: float32 [16384, 128], P('prow'), may hold values from -1.3268871 to 11.326887
- trailing: float32 [16384, 16384], P('prow', 'pcol'), may hold values from -8 to 8
Outputs:
- updated: float32 [16384, 16384], P('prow', 'pcol')
- band_block: float32 [128, 128], replicated
The draws below stay inside these ranges and needn't reach their ends.
All inputs are finite; a program needn't handle non-finite values.
Results may differ from the reference program's by a relative error of at most 0.00012.
Values sent between devices are 32-bit elements; how exact they have to be, the bound alone decides.
No kernel may reach another device: no remote copies, remote signals or barrier semaphores. Data moves between devices by JAX's collectives and lax.ppermute only.
A program may use at most 128 MiB of HBM per device.

```python
import jax
import jax.numpy as jnp
from jax import lax

PANEL = 128
ORDER = 16384


def draw_panel(key, part):
    keys = jax.random.split(jax.random.fold_in(key, 11), 3)
    position = jnp.arange(ORDER, dtype=jnp.float32) / ORDER
    row_scale = jnp.power(3.0, position) * jnp.power(10.0, jax.random.uniform(keys[0], (ORDER,), jnp.float32))
    col_scale = jnp.power(10.0, jax.random.uniform(keys[1], (PANEL,), jnp.float32))
    rough = jnp.clip(jax.random.normal(keys[2], (ORDER, PANEL), jnp.float32), -5.0, 5.0)
    values = rough * row_scale[:, None] * col_scale[None, :] / jnp.sqrt(78.0 * ORDER)
    rows = jnp.arange(ORDER)[:, None]
    cols = jnp.arange(PANEL)[None, :]
    values = values + jnp.where(rows == cols, col_scale[None, :], 0.0)
    return values.astype(jnp.float32)


def draw_trailing(key, part):
    inner = jax.random.fold_in(key, 23)
    source = jnp.clip(jax.random.normal(inner, (ORDER, ORDER), jnp.float32), -5.0, 5.0)
    return ((source + source.T) * 0.7071).astype(jnp.float32)


def setup_inputs(seed: int = 0) -> dict:
    seeds = jax.random.split(jax.random.key(seed), 3)
    return {
        "panel": draw_panel(jax.random.fold_in(seeds[2], 71), 0),
        "trailing": draw_trailing(jax.random.fold_in(seeds[2], 71), 0),
    }


def hdot(left, right):
    return jnp.dot(left.astype(jnp.float32), right.astype(jnp.float32), precision=lax.Precision.HIGHEST, preferred_element_type=jnp.float32)

def reference(panel, trailing):
    gram = hdot(panel.T, panel)
    lower = jnp.linalg.cholesky(gram)
    basis = jax.scipy.linalg.solve_triangular(lower, panel.T, lower=True).T
    head = basis[:PANEL]
    identity_mat = jnp.eye(PANEL, dtype=jnp.float32)
    coupling = jnp.linalg.solve(identity_mat + head.T, identity_mat)
    unit = jnp.concatenate([identity_mat, jnp.zeros((ORDER - PANEL, PANEL), jnp.float32)], axis=0)
    vectors = basis + unit
    mixed = hdot(hdot(trailing, vectors), coupling)
    small = hdot(coupling.T, hdot(vectors.T, mixed))
    update = mixed - 0.5 * hdot(vectors, small)
    updated = trailing - hdot(vectors, update.T) - hdot(update, vectors.T)
    return (updated, -lower.T)
```

```python
import functools

import jax
import jax.numpy as jnp
from jax import lax
from jax.experimental import pallas as pl
from jax.experimental.pallas import tpu as pltpu
from jax.sharding import PartitionSpec as P

B = 128
ZN, XN, YN, CN = 4, 4, 4, 2
F32, BF16 = jnp.float32, jnp.bfloat16
VMEM_LIMIT = 48 * 1024 * 1024


def hdot(left, right, dims=((1,), (0,))):
    return lax.dot_general(
        left, right, (dims, ((), ())), precision=lax.Precision.HIGHEST, preferred_element_type=F32
    )


def bdot(left, right, dims=((1,), (0,))):
    return lax.dot_general(left, right, (dims, ((), ())), preferred_element_type=F32)


def split(value):
    high = value.astype(BF16)
    return high, (value - high.astype(F32)).astype(BF16)


def iotas(shape=(B, B)):
    return lax.broadcasted_iota(jnp.int32, shape, 0), lax.broadcasted_iota(jnp.int32, shape, 1)


def eye():
    r, c = iotas()
    return jnp.where(r == c, 1.0, 0.0).astype(F32)


def params(**kw):
    return pltpu.CompilerParams(vmem_limit_bytes=VMEM_LIMIT, **kw)


STEPS = 6


def inverse_factor(gram, out_ref, s_ref, x_ref):
    r, c = iotas()
    one = eye()
    diag_row = jnp.sum(one * gram, axis=0, keepdims=True)
    diag_col = jnp.sum(one * gram, axis=1, keepdims=True)
    scale_row, scale_col = lax.rsqrt(diag_row), lax.rsqrt(diag_col)
    corr = gram * scale_row * scale_col
    x = one
    err = corr - one
    for step in range(STEPS):
        if step:
            err = hdot(hdot(x, corr), x, ((1,), (1,))) - one
        phi = jnp.where(r > c, err, jnp.where(r == c, 0.5 * err, 0.0))
        x = x - (phi if step == 0 else hdot(phi, x))
    out_ref[...] = x * scale_row
    size = jnp.sum(err * err)
    good = size < 1e-8

    @pl.when(jnp.logical_not(good))
    def _():
        s_ref[...] = corr
        x_ref[...] = one

        def body(k, carry):
            row = s_ref[pl.ds(k, 1), :]
            rr, cc = iotas()
            ident = rr == cc
            lane = lax.broadcasted_iota(jnp.int32, (1, B), 1)
            pivot = jnp.sum(jnp.where(lane == k, row, 0.0), axis=1, keepdims=True)
            inv = lax.rsqrt(pivot)
            row = row * inv
            col = jnp.sum(jnp.where(ident, jnp.broadcast_to(row, (B, B)), 0.0), axis=1, keepdims=True)
            below = lax.broadcasted_iota(jnp.int32, (B, 1), 0) > k
            col = jnp.where(below, col, 0.0)
            xrow = x_ref[pl.ds(k, 1), :] * inv
            x_ref[pl.ds(k, 1), :] = xrow
            s_ref[...] = s_ref[...] - col * row
            x_ref[...] = x_ref[...] - col * xrow
            return carry

        lax.fori_loop(0, B, body, 0)
        out_ref[...] = x_ref[...] * scale_row


def gram_kernel(panel, row_place):
    def body(place_ref, p_ref, out_ref):
        p = p_ref[...]
        out_ref[:, :B] = hdot(p, p, ((0,), (0,)))
        out_ref[:, B:] = jnp.where(place_ref[0] == 0, p[:B], 0.0)

    return pl.pallas_call(
        body,
        out_shape=jax.ShapeDtypeStruct((B, 2 * B), F32),
        in_specs=[pl.BlockSpec(memory_space=pltpu.SMEM), pl.BlockSpec(memory_space=pltpu.VMEM)],
        out_specs=pl.BlockSpec(memory_space=pltpu.VMEM),
        compiler_params=params(),
        name="gram",
    )(row_place, panel)


def product_kernel(panel, trailing):
    rows, cols = trailing.shape
    tile = 256

    def body(p_ref, a_ref, out_ref, ph_ref):
        @pl.when(pl.program_id(0) == 0)
        def _():
            high, low = split(p_ref[...].T)
            ph_ref[:B], ph_ref[B:] = high, low

        ah, al = split(a_ref[...])
        both = bdot(ph_ref[...], ah)
        z = both[:B] + (both[B:] + bdot(ph_ref[:B], al))
        for k in range(tile // B):
            out_ref[k] = z[:, k * B : (k + 1) * B]

    return pl.pallas_call(
        body,
        grid=(cols // tile,),
        out_shape=jax.ShapeDtypeStruct((cols // B, B, B), F32),
        in_specs=[
            pl.BlockSpec((rows, B), lambda t: (0, 0)),
            pl.BlockSpec((rows, tile), lambda t: (0, t)),
        ],
        out_specs=pl.BlockSpec((tile // B, B, B), lambda t: (t, 0, 0)),
        scratch_shapes=[pltpu.VMEM((2 * B, rows), BF16)],
        compiler_params=params(),
        cost_estimate=pl.CostEstimate(flops=6 * rows * cols * B, bytes_accessed=4 * rows * cols, transcendentals=0),
        name="product",
    )(panel, trailing)


def factor_kernel(parts):
    def body(a_ref, b_ref, c_ref, d_ref, band_ref, rinv_ref, head_ref, linv_ref, s_ref, x_ref):
        total = (a_ref[...] + c_ref[...]) + (b_ref[...] + d_ref[...])
        gram, top = total[:, :B], total[:, B:]
        inverse_factor(gram, linv_ref, s_ref, x_ref)
        linv = linv_ref[...]
        rinv = linv.T
        rinv_ref[...] = rinv
        head_ref[...] = hdot(top, rinv)
        r, c = iotas()
        upper = hdot(linv, gram)
        band_ref[...] = jnp.where(r <= c, -upper, -0.0)

    square = jax.ShapeDtypeStruct((B, B), F32)
    return pl.pallas_call(
        body,
        out_shape=(square, square, square),
        scratch_shapes=[pltpu.VMEM((B, B), F32)] * 3,
        compiler_params=params(),
        name="factor",
    )(*parts)


def coupling_kernel(head):
    def body(h_ref, out_ref, linv_ref, s_ref, x_ref):
        m = eye() + h_ref[...].T
        inverse_factor(hdot(m, m, ((0,), (0,))), linv_ref, s_ref, x_ref)
        linv = linv_ref[...]
        out_ref[...] = hdot(linv, hdot(linv, m, ((1,), (1,))), ((0,), (0,)))

    return pl.pallas_call(
        body,
        out_shape=jax.ShapeDtypeStruct((B, B), F32),
        scratch_shapes=[pltpu.VMEM((B, B), F32)] * 3,
        compiler_params=params(),
        name="coupling",
    )(head)


def chunk_kernel(pieces, pa, rinv, first):
    def body(first_ref, y_ref, pa_ref, r_ref, wv_ref, s_ref):
        total = y_ref[0]
        for k in range(1, y_ref.shape[0]):
            total = total + y_ref[k]
        rinv = r_ref[...]
        w = hdot(total, rinv, ((0,), (0,))) + pa_ref[:, B:]
        v = hdot(pa_ref[:, :B], rinv) + jnp.where(first_ref[0] == 1, eye(), 0.0)
        wv_ref[:, :B] = w
        wv_ref[:, B:] = v
        s_ref[...] = hdot(v, w, ((0,), (0,)))

    vm = pl.BlockSpec(memory_space=pltpu.VMEM)
    return pl.pallas_call(
        body,
        out_shape=(jax.ShapeDtypeStruct((B, 2 * B), F32), jax.ShapeDtypeStruct((B, B), F32)),
        in_specs=[pl.BlockSpec(memory_space=pltpu.SMEM), vm, vm, vm],
        out_specs=(vm, vm),
        compiler_params=params(),
        name="chunk",
    )(first, pieces, pa, rinv)


def left_kernel(panel, w_rows, rinv, coupling, s_a, s_b, row_place):
    rows = panel.shape[0]

    def body(place_ref, p_ref, w_ref, r_ref, t_ref, sa_ref, sb_ref, hi_ref, lo_ref):
        t = t_ref[...]
        small = hdot(hdot(t, sa_ref[...] + sb_ref[...], ((0,), (0,))), t)
        small = 0.5 * (small + small.T)
        r, c = iotas((rows, B))
        unit = jnp.where((r == c) & (place_ref[0] == 0), 1.0, 0.0)
        v = hdot(p_ref[...], r_ref[...]) + unit
        hi_ref[:, :B], lo_ref[:, :B] = split(hdot(v, t, ((1,), (1,))))
        hi_ref[:, B:], lo_ref[:, B:] = split(hdot(w_ref[...], t) - hdot(v, small))

    vm = pl.BlockSpec(memory_space=pltpu.VMEM)
    half = jax.ShapeDtypeStruct((rows, 2 * B), BF16)
    return pl.pallas_call(
        body,
        out_shape=(half, half),
        in_specs=[pl.BlockSpec(memory_space=pltpu.SMEM)] + [vm] * 6,
        out_specs=(vm, vm),
        compiler_params=params(),
        name="left",
    )(row_place, panel, w_rows, rinv, coupling, s_a, s_b)


def update_kernel(trailing, high, low, right):
    rows, cols = trailing.shape
    tile = 256

    def body(a_ref, h_ref, l_ref, r_ref, out_ref):
        rh, rl = split(r_ref[...])
        h = h_ref[...]
        nt = ((1,), (1,))
        out_ref[...] = a_ref[...] - (bdot(h, rh, nt) + (bdot(h, rl, nt) + bdot(l_ref[...], rh, nt)))

    whole = pl.BlockSpec((rows, 2 * B), lambda t: (0, 0))
    return pl.pallas_call(
        body,
        grid=(cols // tile,),
        out_shape=jax.ShapeDtypeStruct((rows, cols), F32),
        in_specs=[
            pl.BlockSpec((rows, tile), lambda t: (0, t)),
            whole,
            whole,
            pl.BlockSpec((tile, 2 * B), lambda t: (t, 0)),
        ],
        out_specs=pl.BlockSpec((rows, tile), lambda t: (0, t)),
        compiler_params=params(),
        cost_estimate=pl.CostEstimate(flops=12 * rows * cols * B, bytes_accessed=8 * rows * cols, transcendentals=0),
        name="update",
    )(trailing, high, low, right)


def along_x(d):
    return [(z * XN + x, z * XN + (x + d) % XN) for z in range(ZN) for x in range(XN)]


def along_z(d):
    return [(z * XN + x, (z + d) % ZN * XN + x) for z in range(ZN) for x in range(XN)]


def along_y(d):
    return [(y * CN + c, (y + d) % YN * CN + c) for y in range(YN) for c in range(CN)]


def along_c(d):
    return [(y * CN + c, y * CN + (c + d) % CN) for y in range(YN) for c in range(CN)]


def four(value, axis, along):
    return [value] + [lax.ppermute(value, axis, along(d)) for d in (1, 2, 3)]


def add_four(parts):
    return (parts[0] + parts[2]) + (parts[1] + parts[3])


def shards(panel, trailing):
    rows, cols = trailing.shape
    prow, pcol = lax.axis_size("prow"), lax.axis_size("pcol")
    i, j = lax.axis_index("prow"), lax.axis_index("pcol")
    row_place = i.astype(jnp.int32).reshape(1)
    first = ((i == 0) & (j == 0)).astype(jnp.int32).reshape(1)
    per_row = rows // B
    ratio = cols // rows

    spread = []
    for a in range(prow):
        for k in range(per_row):
            spread.append((a * pcol + k, (per_row * (a % ratio) + k) * pcol + a // ratio))
    gather = [(d, s) for s, d in spread]

    parts = four(gram_kernel(panel, row_place), "prow", along_x)
    parts = four(add_four(parts), "prow", along_z)

    z = product_kernel(panel, trailing)
    pieces = lax.all_to_all(z, "prow", split_axis=0, concat_axis=0, tiled=True)

    lead = trailing[:, :B].reshape(YN, CN, B, B)
    held = jnp.where(j == 0, lead[:, 0], lax.ppermute(lead[:, 1], "pcol", [(0, 1)]))
    sent = [lax.ppermute(held[y], "pcol", [(c, y * CN + c) for c in range(CN)]) for y in range(1, YN)]
    ae = jnp.where(j < CN, held[0], sent[0] + sent[1] + sent[2])
    mine = lax.dynamic_slice_in_dim(panel, j * B, B, 0)
    pa = lax.ppermute(jnp.concatenate([mine, ae], axis=1), ("prow", "pcol"), spread)

    band, rinv, head = factor_kernel(parts)
    wv, s = chunk_kernel(pieces, pa, rinv, first)

    copies = jnp.broadcast_to(wv, (prow, B, 2 * B))
    right = lax.all_to_all(copies, "prow", split_axis=0, concat_axis=0, tiled=True).reshape(cols, 2 * B)
    w_row = lax.ppermute(wv[:, :B], ("prow", "pcol"), gather)
    copies = jnp.broadcast_to(w_row, (pcol, B, B))
    w_rows = lax.all_to_all(copies, "pcol", split_axis=0, concat_axis=0, tiled=True).reshape(rows, B)

    coupling = coupling_kernel(head)
    s = add_four(four(s, "prow", along_x))
    s = add_four(four(s, "prow", along_z))
    s = add_four(four(s, "pcol", along_y))
    s_other = lax.ppermute(s, "pcol", along_c(1))
    high, low = left_kernel(panel, w_rows, rinv, coupling, s, s_other, row_place)
    return update_kernel(trailing, high, low, right), band


def solution(mesh):
    placed = (P("prow", None), P("prow", "pcol"))
    return jax.shard_map(
        shards, mesh=mesh, in_specs=placed, out_specs=(P("prow", "pcol"), P()), check_vma=False
    )
```

```python
import jax
import jax.numpy as jnp
from jax import lax
from jax.experimental import pallas as pl
from jax.experimental.pallas import tpu as pltpu
from jax.sharding import PartitionSpec as P

B = 128
ZN, XN, YN, CN = 4, 4, 4, 2
F32, BF16 = jnp.float32, jnp.bfloat16
VMEM_LIMIT = 48 * 1024 * 1024


def hdot(left, right, dims=((1,), (0,))):
    return lax.dot_general(
        left, right, (dims, ((), ())), precision=lax.Precision.HIGHEST, preferred_element_type=F32
    )


def bdot(left, right, dims=((1,), (0,))):
    return lax.dot_general(left, right, (dims, ((), ())), preferred_element_type=F32)


def split(value):
    high = value.astype(BF16)
    return high, (value - high.astype(F32)).astype(BF16)


def dot3(left, right, dims=((1,), (0,))):
    (lh, ll), (rh, rl) = split(left), split(right)
    return bdot(lh, rh, dims) + (bdot(lh, rl, dims) + bdot(ll, rh, dims))


def iotas(shape=(B, B)):
    return lax.broadcasted_iota(jnp.int32, shape, 0), lax.broadcasted_iota(jnp.int32, shape, 1)


def eye():
    r, c = iotas()
    return jnp.where(r == c, 1.0, 0.0).astype(F32)


def params(**kw):
    return pltpu.CompilerParams(vmem_limit_bytes=VMEM_LIMIT, **kw)


STEPS = 6


def inverse_factor(gram, out_ref, s_ref, x_ref):
    r, c = iotas()
    one = eye()
    diag_row = jnp.sum(one * gram, axis=0, keepdims=True)
    diag_col = jnp.sum(one * gram, axis=1, keepdims=True)
    scale_row, scale_col = lax.rsqrt(diag_row), lax.rsqrt(diag_col)
    corr = gram * scale_row * scale_col
    x = one
    err = corr - one
    for step in range(STEPS):
        if step:
            err = hdot(hdot(x, corr), x, ((1,), (1,))) - one
        phi = jnp.where(r > c, err, jnp.where(r == c, 0.5 * err, 0.0))
        x = x - (phi if step == 0 else hdot(phi, x))
    out_ref[...] = x * scale_row
    size = jnp.sum(err * err)
    good = size < 1e-8

    @pl.when(jnp.logical_not(good))
    def _():
        s_ref[...] = corr
        x_ref[...] = one

        def body(k, carry):
            row = s_ref[pl.ds(k, 1), :]
            rr, cc = iotas()
            ident = rr == cc
            lane = lax.broadcasted_iota(jnp.int32, (1, B), 1)
            pivot = jnp.sum(jnp.where(lane == k, row, 0.0), axis=1, keepdims=True)
            inv = lax.rsqrt(pivot)
            row = row * inv
            col = jnp.sum(jnp.where(ident, jnp.broadcast_to(row, (B, B)), 0.0), axis=1, keepdims=True)
            below = lax.broadcasted_iota(jnp.int32, (B, 1), 0) > k
            col = jnp.where(below, col, 0.0)
            xrow = x_ref[pl.ds(k, 1), :] * inv
            x_ref[pl.ds(k, 1), :] = xrow
            s_ref[...] = s_ref[...] - col * row
            x_ref[...] = x_ref[...] - col * xrow
            return carry

        lax.fori_loop(0, B, body, 0)
        out_ref[...] = x_ref[...] * scale_row


SMEM = pl.BlockSpec(memory_space=pltpu.SMEM)
VMEM = pl.BlockSpec(memory_space=pltpu.VMEM)


def shaped(*shape, dtype=F32):
    return jax.ShapeDtypeStruct(shape, dtype)


ANY = pl.BlockSpec(memory_space=pl.ANY)


def gram_kernel(panel):
    def body(p_ref, out_ref):
        p = p_ref[...]
        out_ref[...] = hdot(p, p, ((0,), (0,)))

    return pl.pallas_call(body, out_shape=shaped(B, B), compiler_params=params(), name="gram")(panel)


def product_kernel(panel, rinv, trailing, first_row, after):
    rows, cols = trailing.shape
    tile = 1024
    chunks = tile // B

    def body(first_ref, p_ref, r_ref, a_ref, *refs):
        v_ref, out_ref, vh_ref = refs[-3:]

        @pl.when(pl.program_id(0) == 0)
        def _():
            r, c = iotas((rows, B))
            v = dot3(p_ref[...], r_ref[...]) + jnp.where((r == c) & (first_ref[0] == 1), 1.0, 0.0)
            v_ref[...] = v
            vh_ref[:B], vh_ref[B:] = split(v.T)

        ah, al = split(a_ref[...])
        both = bdot(vh_ref[...], ah)
        z = both[:B] + (both[B:] + bdot(vh_ref[:B], al))
        for k in range(chunks):
            out_ref[k, 0] = z[:, k * B : (k + 1) * B]

    return pl.pallas_call(
        body,
        grid=(cols // tile,),
        out_shape=(shaped(rows, B), shaped(chunks, cols // tile, B, B)),
        in_specs=[
            SMEM,
            pl.BlockSpec((rows, B), lambda t: (0, 0)),
            pl.BlockSpec((B, B), lambda t: (0, 0)),
            pl.BlockSpec((rows, tile), lambda t: (0, t)),
        ]
        + [ANY] * len(after),
        out_specs=(
            pl.BlockSpec((rows, B), lambda t: (0, 0)),
            pl.BlockSpec((chunks, 1, B, B), lambda t: (0, t, 0, 0)),
        ),
        scratch_shapes=[pltpu.VMEM((2 * B, rows), BF16)],
        compiler_params=params(),
        cost_estimate=pl.CostEstimate(flops=6 * rows * cols * B, bytes_accessed=4 * rows * cols, transcendentals=0),
        name="product",
    )(first_row, panel, rinv, trailing, *after)


def factor_kernel(parts):
    def body(a_ref, b_ref, c_ref, d_ref, band_ref, rinv_ref, linv_ref, s_ref, x_ref):
        gram = (a_ref[...] + c_ref[...]) + (b_ref[...] + d_ref[...])
        inverse_factor(gram, linv_ref, s_ref, x_ref)
        linv = linv_ref[...]
        rinv_ref[...] = linv.T
        r, c = iotas()
        band_ref[...] = jnp.where(r <= c, -hdot(linv, gram), -0.0)

    square = shaped(B, B)
    return pl.pallas_call(
        body,
        out_shape=(square, square),
        scratch_shapes=[pltpu.VMEM((B, B), F32)] * 3,
        compiler_params=params(),
        name="factor",
    )(*parts)


def chunk_kernel(pieces, after):
    count = pieces.shape[0]

    def body(y_ref, after_ref, w_ref):
        total = [y_ref[k] for k in range(count)]
        while len(total) > 1:
            total = [l + r for l, r in zip(total[::2], total[1::2])]
        w_ref[...] = total[0].T

    return pl.pallas_call(
        body, out_shape=shaped(B, B), in_specs=[VMEM, ANY], compiler_params=params(), name="chunk"
    )(pieces, after)


def copies_kernel(w, v, count, after):
    def body(w_ref, v_ref, after_ref, copies_ref):
        for k in range(count):
            copies_ref[k, :, :B] = w_ref[...]
            copies_ref[k, :, B:] = v_ref[...]

    return pl.pallas_call(
        body, out_shape=shaped(count, B, 2 * B), in_specs=[VMEM, VMEM, ANY], compiler_params=params(), name="copies"
    )(w, v, after)


def small_kernel(right, after):
    rows = right.shape[0] * right.shape[1] * B

    def body(r_ref, after_ref, out_ref):
        both = r_ref[...].reshape(rows, 2 * B)
        out_ref[...] = dot3(both[:, B:], both[:, :B], ((0,), (0,)))

    return pl.pallas_call(
        body, out_shape=shaped(B, B), in_specs=[VMEM, ANY], compiler_params=params(), name="small"
    )(right, after)


def mixed_kernel(w_parts, coupling, place):
    part = w_parts[0].shape[0]

    def body(place_ref, t_ref, *refs):
        part_refs, out_ref = refs[:YN], refs[YN]
        for d in range(YN):
            y = lax.rem(place_ref[1] + (YN - d), YN)
            out_ref[pl.ds(pl.multiple_of(y * part, part), part), :] = dot3(part_refs[d][...], t_ref[...])

    return pl.pallas_call(
        body,
        out_shape=shaped(YN * part, B),
        in_specs=[SMEM] + [VMEM] * (YN + 1),
        compiler_params=params(),
        name="mixed",
    )(place, coupling, *w_parts)


def coupling_kernel(tops, rinv):
    def body(*refs):
        top_refs, (r_ref, out_ref, linv_ref, s_ref, x_ref) = refs[:4], refs[4:]
        top = (top_refs[0][...] + top_refs[1][...]) + (top_refs[2][...] + top_refs[3][...])
        m = eye() + hdot(top, r_ref[...]).T
        inverse_factor(hdot(m, m, ((0,), (0,))), linv_ref, s_ref, x_ref)
        linv = linv_ref[...]
        out_ref[...] = hdot(linv, hdot(linv, m, ((1,), (1,))), ((0,), (0,)))

    return pl.pallas_call(
        body,
        out_shape=shaped(B, B),
        scratch_shapes=[pltpu.VMEM((B, B), F32)] * 3,
        compiler_params=params(),
        name="coupling",
    )(*tops, rinv)


def turned_kernel(v, coupling):
    def body(v_ref, t_ref, h_ref, l_ref):
        h_ref[...], l_ref[...] = split(dot3(v_ref[...], t_ref[...], ((1,), (1,))))

    half = shaped(*v.shape, dtype=BF16)
    return pl.pallas_call(body, out_shape=(half, half), compiler_params=params(), name="turned")(v, coupling)


def update_kernel(trailing, right, v, turned, mixed, coupling, parts):
    rows, cols = trailing.shape
    tile = 512
    chunks = tile // B

    def body(a_ref, right_ref, v_ref, th_ref, tl_ref, m_ref, t_ref, *refs):
        s_refs, (out_ref, h_ref, l_ref) = refs[:YN], refs[YN:]

        @pl.when(pl.program_id(0) == 0)
        def _():
            t = t_ref[...]
            s = [ref[...] for ref in s_refs]
            small = hdot(hdot(t, (s[0] + s[2]) + (s[1] + s[3]), ((0,), (0,))), t)
            small = 0.5 * (small + small.T)
            h_ref[:, :B], l_ref[:, :B] = th_ref[...], tl_ref[...]
            h_ref[:, B:], l_ref[:, B:] = split(m_ref[...] - dot3(v_ref[...], small))

        rh, rl = split(right_ref[...].reshape(tile, 2 * B))
        h = h_ref[...]
        nt = ((1,), (1,))
        out_ref[...] = a_ref[...] - (bdot(h, rh, nt) + (bdot(h, rl, nt) + bdot(l_ref[...], rh, nt)))

    def whole(*shape):
        return pl.BlockSpec(shape, lambda t: (0, 0))

    per_half = right.shape[0] // chunks
    return pl.pallas_call(
        body,
        grid=(cols // tile,),
        out_shape=shaped(rows, cols),
        in_specs=[
            pl.BlockSpec((rows, tile), lambda t: (0, t)),
            pl.BlockSpec((chunks, 1, B, 2 * B), lambda t: (t % per_half, t // per_half, 0, 0)),
            whole(rows, B),
            whole(rows, B),
            whole(rows, B),
            whole(rows, B),
            whole(B, B),
        ]
        + [whole(B, B)] * YN,
        out_specs=pl.BlockSpec((rows, tile), lambda t: (0, t)),
        scratch_shapes=[pltpu.VMEM((rows, 2 * B), BF16)] * 2,
        compiler_params=params(),
        cost_estimate=pl.CostEstimate(flops=12 * rows * cols * B, bytes_accessed=8 * rows * cols, transcendentals=0),
        name="update",
    )(trailing, right, v, *turned, mixed, coupling, *parts)


def along_x(d):
    return [(z * XN + x, z * XN + (x + d) % XN) for z in range(ZN) for x in range(XN)]


def along_z(d):
    return [(z * XN + x, (z + d) % ZN * XN + x) for z in range(ZN) for x in range(XN)]


def along_y(d):
    return [(y * CN + c, (y + d) % YN * CN + c) for y in range(YN) for c in range(CN)]


def along_c(d):
    return [(y * CN + c, y * CN + (c + d) % CN) for y in range(YN) for c in range(CN)]


def four(value, axis, along):
    return [value] + [lax.ppermute(value, axis, along(d)) for d in (1, 2, 3)]


def add_four(parts):
    return (parts[0] + parts[2]) + (parts[1] + parts[3])


def to_all(copies, axis):
    return lax.all_to_all(copies, axis, split_axis=0, concat_axis=0, tiled=True)


def shards(panel, trailing):
    rows, cols = trailing.shape
    prow = lax.axis_size("prow")
    i, j = lax.axis_index("prow"), lax.axis_index("pcol")
    y, c, x = j // CN, j % CN, i % XN
    place = jnp.stack([i, y]).astype(jnp.int32)
    first_row = (i == 0).astype(jnp.int32).reshape(1)

    def device(z, x, y, c):
        return ((z * XN + x) * YN + y) * CN + c

    coords = [(z, x, y, c) for z in range(ZN) for x in range(XN) for y in range(YN) for c in range(CN)]
    swap = [(device(y, 2 * c + x % 2, z, x // 2), device(z, x, y, c)) for z, x, y, c in coords]

    top = jnp.where(i == 0, panel[:B], jnp.zeros_like(panel[:B]))
    parts = four(gram_kernel(panel), "prow", along_x)
    top = top + sum(lax.ppermute(top, "prow", [(0, k)]) for k in range(1, XN))
    parts = four(add_four(parts), "prow", along_z)
    tops = [top] + [lax.ppermute(top, "prow", [(k, z * XN + k) for k in range(XN)]) for z in range(1, ZN)]
    band, rinv = factor_kernel(parts)
    v, chunks = product_kernel(panel, rinv, trailing, first_row, tops)
    pieces = to_all(chunks.reshape(prow, B, B), "prow")

    v_chunk = lax.ppermute(lax.dynamic_slice_in_dim(v, j * B, B, 0), ("prow", "pcol"), swap)
    tops[0], _ = lax.optimization_barrier((tops[0], v))
    coupling = coupling_kernel(tops, rinv)
    turned = turned_kernel(v, coupling)

    w = chunk_kernel(pieces, turned[0])
    row_w = lax.ppermute(w, ("prow", "pcol"), swap)
    right = to_all(copies_kernel(w, v_chunk, prow, row_w), "prow").reshape(*chunks.shape[:3], 2 * B)

    other = lax.ppermute(row_w, "pcol", along_c(1))
    row_w = jnp.concatenate([jnp.where(c == 0, row_w, other), jnp.where(c == 0, other, row_w)])
    mixed = mixed_kernel(four(row_w, "pcol", along_y), coupling, place)

    part = small_kernel(right, mixed)
    part = part + lax.ppermute(part, "pcol", along_c(1))
    parts = four(part, "pcol", along_y)
    return update_kernel(trailing, right, v, turned, mixed, coupling, parts), band


def solution(mesh):
    placed = (P("prow", None), P("prow", "pcol"))
    return jax.shard_map(
        shards, mesh=mesh, in_specs=placed, out_specs=(P("prow", "pcol"), P()), check_vma=False
    )
```

```python
import jax
import jax.numpy as jnp
from jax import lax
from jax.experimental import pallas as pl
from jax.experimental.pallas import tpu as pltpu
from jax.sharding import PartitionSpec as P

B = 128
ZN, XN, YN, CN = 4, 4, 4, 2
F32, BF16 = jnp.float32, jnp.bfloat16
VMEM_LIMIT = 48 * 1024 * 1024


def hdot(left, right, dims=((1,), (0,))):
    return lax.dot_general(
        left, right, (dims, ((), ())), precision=lax.Precision.HIGHEST, preferred_element_type=F32
    )


def bdot(left, right, dims=((1,), (0,))):
    return lax.dot_general(left, right, (dims, ((), ())), preferred_element_type=F32)


def split(value):
    high = value.astype(BF16)
    return high, (value - high.astype(F32)).astype(BF16)


def dot3(left, right, dims=((1,), (0,))):
    (lh, ll), (rh, rl) = split(left), split(right)
    return bdot(lh, rh, dims) + (bdot(lh, rl, dims) + bdot(ll, rh, dims))


def iotas(shape=(B, B)):
    return lax.broadcasted_iota(jnp.int32, shape, 0), lax.broadcasted_iota(jnp.int32, shape, 1)


def eye():
    r, c = iotas()
    return jnp.where(r == c, 1.0, 0.0).astype(F32)


def params(**kw):
    return pltpu.CompilerParams(vmem_limit_bytes=VMEM_LIMIT, **kw)


STEPS = 6


def inverse_factor(gram, out_ref, s_ref, x_ref):
    r, c = iotas()
    one = eye()
    diag_row = jnp.sum(one * gram, axis=0, keepdims=True)
    diag_col = jnp.sum(one * gram, axis=1, keepdims=True)
    scale_row, scale_col = lax.rsqrt(diag_row), lax.rsqrt(diag_col)
    corr = gram * scale_row * scale_col
    x = one
    err = corr - one
    for step in range(STEPS):
        dot = hdot if step >= STEPS - 2 else dot3
        if step:
            err = dot(dot(x, corr), x, ((1,), (1,))) - one
        phi = jnp.where(r > c, err, jnp.where(r == c, 0.5 * err, 0.0))
        x = x - (phi if step == 0 else dot(phi, x))
    out_ref[...] = x * scale_row
    size = jnp.sum(err * err)
    good = size < 1e-8

    @pl.when(jnp.logical_not(good))
    def _():
        s_ref[...] = corr
        x_ref[...] = one

        def body(k, carry):
            row = s_ref[pl.ds(k, 1), :]
            rr, cc = iotas()
            ident = rr == cc
            lane = lax.broadcasted_iota(jnp.int32, (1, B), 1)
            pivot = jnp.sum(jnp.where(lane == k, row, 0.0), axis=1, keepdims=True)
            inv = lax.rsqrt(pivot)
            row = row * inv
            col = jnp.sum(jnp.where(ident, jnp.broadcast_to(row, (B, B)), 0.0), axis=1, keepdims=True)
            below = lax.broadcasted_iota(jnp.int32, (B, 1), 0) > k
            col = jnp.where(below, col, 0.0)
            xrow = x_ref[pl.ds(k, 1), :] * inv
            x_ref[pl.ds(k, 1), :] = xrow
            s_ref[...] = s_ref[...] - col * row
            x_ref[...] = x_ref[...] - col * xrow
            return carry

        lax.fori_loop(0, B, body, 0)
        out_ref[...] = x_ref[...] * scale_row


SMEM = pl.BlockSpec(memory_space=pltpu.SMEM)
VMEM = pl.BlockSpec(memory_space=pltpu.VMEM)


def shaped(*shape, dtype=F32):
    return jax.ShapeDtypeStruct(shape, dtype)


ANY = pl.BlockSpec(memory_space=pl.ANY)


def gram_kernel(panel):
    def body(p_ref, out_ref):
        p = p_ref[...]
        out_ref[...] = hdot(p, p, ((0,), (0,)))

    return pl.pallas_call(body, out_shape=shaped(B, B), compiler_params=params(), name="gram")(panel)


def product_kernel(panel, rinv, trailing, first_row, after):
    rows, cols = trailing.shape
    tile = 1024
    chunks = tile // B

    def body(first_ref, p_ref, r_ref, a_ref, *refs):
        v_ref, out_ref, vh_ref = refs[-3:]

        @pl.when(pl.program_id(0) == 0)
        def _():
            r, c = iotas((rows, B))
            v = dot3(p_ref[...], r_ref[...]) + jnp.where((r == c) & (first_ref[0] == 1), 1.0, 0.0)
            v_ref[...] = v
            vh_ref[:B], vh_ref[B:] = split(v.T)

        ah, al = split(a_ref[...])
        both = bdot(vh_ref[...], ah)
        z = both[:B] + (both[B:] + bdot(vh_ref[:B], al))
        for k in range(chunks):
            out_ref[k, 0] = z[:, k * B : (k + 1) * B]

    return pl.pallas_call(
        body,
        grid=(cols // tile,),
        out_shape=(shaped(rows, B), shaped(chunks, cols // tile, B, B)),
        in_specs=[
            SMEM,
            pl.BlockSpec((rows, B), lambda t: (0, 0)),
            pl.BlockSpec((B, B), lambda t: (0, 0)),
            pl.BlockSpec((rows, tile), lambda t: (0, t)),
        ]
        + [ANY] * len(after),
        out_specs=(
            pl.BlockSpec((rows, B), lambda t: (0, 0)),
            pl.BlockSpec((chunks, 1, B, B), lambda t: (0, t, 0, 0)),
        ),
        scratch_shapes=[pltpu.VMEM((2 * B, rows), BF16)],
        compiler_params=params(),
        cost_estimate=pl.CostEstimate(flops=6 * rows * cols * B, bytes_accessed=4 * rows * cols, transcendentals=0),
        name="product",
    )(first_row, panel, rinv, trailing, *after)


def factor_kernel(parts):
    def body(a_ref, b_ref, c_ref, d_ref, band_ref, rinv_ref, linv_ref, s_ref, x_ref):
        gram = (a_ref[...] + c_ref[...]) + (b_ref[...] + d_ref[...])
        inverse_factor(gram, linv_ref, s_ref, x_ref)
        linv = linv_ref[...]
        rinv_ref[...] = linv.T
        r, c = iotas()
        band_ref[...] = jnp.where(r <= c, -hdot(linv, gram), -0.0)

    square = shaped(B, B)
    return pl.pallas_call(
        body,
        out_shape=(square, square),
        scratch_shapes=[pltpu.VMEM((B, B), F32)] * 3,
        compiler_params=params(),
        name="factor",
    )(*parts)


def chunk_kernel(pieces, after):
    count = pieces.shape[0]

    def body(y_ref, after_ref, w_ref):
        total = [y_ref[k] for k in range(count)]
        while len(total) > 1:
            total = [l + r for l, r in zip(total[::2], total[1::2])]
        w_ref[...] = total[0].T

    return pl.pallas_call(
        body, out_shape=shaped(B, B), in_specs=[VMEM, ANY], compiler_params=params(), name="chunk"
    )(pieces, after)


def copies_kernel(w, v, count, after):
    def body(w_ref, v_ref, after_ref, copies_ref):
        for k in range(count):
            copies_ref[k, :, :B] = w_ref[...]
            copies_ref[k, :, B:] = v_ref[...]

    return pl.pallas_call(
        body, out_shape=shaped(count, B, 2 * B), in_specs=[VMEM, VMEM, ANY], compiler_params=params(), name="copies"
    )(w, v, after)


def small_kernel(right, after):
    rows = right.shape[0] * right.shape[1] * B

    def body(r_ref, after_ref, out_ref):
        both = r_ref[...].reshape(rows, 2 * B)
        out_ref[...] = dot3(both[:, B:], both[:, :B], ((0,), (0,)))

    return pl.pallas_call(
        body, out_shape=shaped(B, B), in_specs=[VMEM, ANY], compiler_params=params(), name="small"
    )(right, after)


def mixed_kernel(w_parts, coupling, place):
    part = w_parts[0].shape[0]

    def body(place_ref, t_ref, *refs):
        part_refs, out_ref = refs[:YN], refs[YN]
        for d in range(YN):
            y = lax.rem(place_ref[1] + (YN - d), YN)
            out_ref[pl.ds(pl.multiple_of(y * part, part), part), :] = dot3(part_refs[d][...], t_ref[...])

    return pl.pallas_call(
        body,
        out_shape=shaped(YN * part, B),
        in_specs=[SMEM] + [VMEM] * (YN + 1),
        compiler_params=params(),
        name="mixed",
    )(place, coupling, *w_parts)


def coupling_kernel(tops, rinv):
    def body(*refs):
        top_refs, (r_ref, out_ref, linv_ref, s_ref, x_ref) = refs[:4], refs[4:]
        top = (top_refs[0][...] + top_refs[1][...]) + (top_refs[2][...] + top_refs[3][...])
        m = eye() + hdot(top, r_ref[...]).T
        inverse_factor(hdot(m, m, ((0,), (0,))), linv_ref, s_ref, x_ref)
        linv = linv_ref[...]
        out_ref[...] = hdot(linv, hdot(linv, m, ((1,), (1,))), ((0,), (0,)))

    return pl.pallas_call(
        body,
        out_shape=shaped(B, B),
        scratch_shapes=[pltpu.VMEM((B, B), F32)] * 3,
        compiler_params=params(),
        name="coupling",
    )(*tops, rinv)


def turned_kernel(v, coupling):
    def body(v_ref, t_ref, h_ref, l_ref):
        h_ref[...], l_ref[...] = split(dot3(v_ref[...], t_ref[...], ((1,), (1,))))

    half = shaped(*v.shape, dtype=BF16)
    return pl.pallas_call(body, out_shape=(half, half), compiler_params=params(), name="turned")(v, coupling)


def update_kernel(trailing, right, v, turned, mixed, coupling, parts):
    rows, cols = trailing.shape
    tile = rows // 2
    halves = right.shape[1]
    wide = cols // halves

    def body(a_ref, right_ref, v_ref, th_ref, tl_ref, m_ref, t_ref, *refs):
        s_refs, (out_ref, small_ref, rh_ref, rl_ref) = refs[:YN], refs[YN:]

        @pl.when(pl.program_id(0) == 0)
        def _():
            t = t_ref[...]
            s = [ref[...] for ref in s_refs]
            small = hdot(hdot(t, (s[0] + s[2]) + (s[1] + s[3]), ((0,), (0,))), t)
            small_ref[...] = 0.5 * (small + small.T)
            for h in range(halves):
                at = slice(h * wide, (h + 1) * wide)
                rh_ref[at], rl_ref[at] = split(right_ref[:, h].reshape(wide, 2 * B))

        high, low = split(m_ref[...] - dot3(v_ref[...], small_ref[...]))
        high = jnp.concatenate([th_ref[...], high], axis=1)
        low = jnp.concatenate([tl_ref[...], low], axis=1)
        nt = ((1,), (1,))
        for k in range(0, cols, 512):
            at = slice(k, k + 512)
            rh, rl = rh_ref[at], rl_ref[at]
            out_ref[:, at] = a_ref[:, at] - (bdot(high, rh, nt) + (bdot(high, rl, nt) + bdot(low, rh, nt)))

    def whole(*shape):
        return pl.BlockSpec(shape, lambda t: (0,) * len(shape))

    def mine(width):
        return pl.BlockSpec((tile, width), lambda t: (t, 0))

    return pl.pallas_call(
        body,
        grid=(rows // tile,),
        out_shape=shaped(rows, cols),
        in_specs=[mine(cols), whole(*right.shape), mine(B), mine(B), mine(B), mine(B), whole(B, B)] + [whole(B, B)] * YN,
        out_specs=mine(cols),
        scratch_shapes=[pltpu.VMEM((B, B), F32)] + [pltpu.VMEM((cols, 2 * B), BF16)] * 2,
        compiler_params=params(),
        cost_estimate=pl.CostEstimate(flops=12 * rows * cols * B, bytes_accessed=8 * rows * cols, transcendentals=0),
        name="update",
    )(trailing, right, v, *turned, mixed, coupling, *parts)


def along_x(d):
    return [(z * XN + x, z * XN + (x + d) % XN) for z in range(ZN) for x in range(XN)]


def along_z(d):
    return [(z * XN + x, (z + d) % ZN * XN + x) for z in range(ZN) for x in range(XN)]


def along_y(d):
    return [(y * CN + c, (y + d) % YN * CN + c) for y in range(YN) for c in range(CN)]


def along_c(d):
    return [(y * CN + c, y * CN + (c + d) % CN) for y in range(YN) for c in range(CN)]


def four(value, axis, along):
    return [value] + [lax.ppermute(value, axis, along(d)) for d in (1, 2, 3)]


def add_four(parts):
    return (parts[0] + parts[2]) + (parts[1] + parts[3])


def to_all(copies, axis):
    return lax.all_to_all(copies, axis, split_axis=0, concat_axis=0, tiled=True)


def shards(panel, trailing):
    rows, cols = trailing.shape
    prow = lax.axis_size("prow")
    i, j = lax.axis_index("prow"), lax.axis_index("pcol")
    y, c, x = j // CN, j % CN, i % XN
    place = jnp.stack([i, y]).astype(jnp.int32)
    first_row = (i == 0).astype(jnp.int32).reshape(1)

    def device(z, x, y, c):
        return ((z * XN + x) * YN + y) * CN + c

    coords = [(z, x, y, c) for z in range(ZN) for x in range(XN) for y in range(YN) for c in range(CN)]
    swap = [(device(y, 2 * c + x % 2, z, x // 2), device(z, x, y, c)) for z, x, y, c in coords]

    top = jnp.where(i == 0, panel[:B], jnp.zeros_like(panel[:B]))
    parts = four(gram_kernel(panel), "prow", along_x)
    top = top + sum(lax.ppermute(top, "prow", [(0, k)]) for k in range(1, XN))
    parts = four(add_four(parts), "prow", along_z)
    tops = [top] + [lax.ppermute(top, "prow", [(k, z * XN + k) for k in range(XN)]) for z in range(1, ZN)]
    band, rinv = factor_kernel(parts)
    v, chunks = product_kernel(panel, rinv, trailing, first_row, tops)
    pieces = to_all(chunks.reshape(prow, B, B), "prow")

    v_chunk = lax.ppermute(lax.dynamic_slice_in_dim(v, j * B, B, 0), ("prow", "pcol"), swap)
    tops[0], _ = lax.optimization_barrier((tops[0], v))
    coupling = coupling_kernel(tops, rinv)
    turned = turned_kernel(v, coupling)

    w = chunk_kernel(pieces, turned[0])
    row_w = lax.ppermute(w, ("prow", "pcol"), swap)
    right = to_all(copies_kernel(w, v_chunk, prow, row_w), "prow").reshape(*chunks.shape[:3], 2 * B)

    other = lax.ppermute(row_w, "pcol", along_c(1))
    row_w = jnp.concatenate([jnp.where(c == 0, row_w, other), jnp.where(c == 0, other, row_w)])
    mixed = mixed_kernel(four(row_w, "pcol", along_y), coupling, place)

    part = small_kernel(right, mixed)
    part = part + lax.ppermute(part, "pcol", along_c(1))
    parts = four(part, "pcol", along_y)
    return update_kernel(trailing, right, v, turned, mixed, coupling, parts), band


def solution(mesh):
    placed = (P("prow", None), P("prow", "pcol"))
    return jax.shard_map(
        shards, mesh=mesh, in_specs=placed, out_specs=(P("prow", "pcol"), P()), check_vma=False
    )
```

```python
import jax
import jax.numpy as jnp
from jax import lax
from jax.experimental import pallas as pl
from jax.experimental.pallas import tpu as pltpu
from jax.sharding import PartitionSpec as P

B = 128
ZN, XN, YN, CN = 4, 4, 4, 2
F32, BF16 = jnp.float32, jnp.bfloat16
VMEM_LIMIT = 48 * 1024 * 1024


def hdot(left, right, dims=((1,), (0,))):
    return lax.dot_general(
        left, right, (dims, ((), ())), precision=lax.Precision.HIGHEST, preferred_element_type=F32
    )


def bdot(left, right, dims=((1,), (0,))):
    return lax.dot_general(left, right, (dims, ((), ())), preferred_element_type=F32)


def split(value):
    high = value.astype(BF16)
    return high, (value - high.astype(F32)).astype(BF16)


def dot3(left, right, dims=((1,), (0,))):
    (lh, ll), (rh, rl) = split(left), split(right)
    return bdot(lh, rh, dims) + (bdot(lh, rl, dims) + bdot(ll, rh, dims))


def iotas(shape=(B, B)):
    return lax.broadcasted_iota(jnp.int32, shape, 0), lax.broadcasted_iota(jnp.int32, shape, 1)


def eye():
    r, c = iotas()
    return jnp.where(r == c, 1.0, 0.0).astype(F32)


def params(**kw):
    return pltpu.CompilerParams(vmem_limit_bytes=VMEM_LIMIT, **kw)


STEPS = 6


def inverse_factor(gram, out_ref, s_ref, x_ref):
    r, c = iotas()
    one = eye()
    diag_row = jnp.sum(one * gram, axis=0, keepdims=True)
    diag_col = jnp.sum(one * gram, axis=1, keepdims=True)
    scale_row, scale_col = lax.rsqrt(diag_row), lax.rsqrt(diag_col)
    corr = gram * scale_row * scale_col
    x = one
    err = corr - one
    for step in range(STEPS):
        dot = hdot if step >= STEPS - 2 else dot3
        if step:
            err = dot(dot(x, corr), x, ((1,), (1,))) - one
        phi = jnp.where(r > c, err, jnp.where(r == c, 0.5 * err, 0.0))
        x = x - (phi if step == 0 else dot(phi, x))
    out_ref[...] = x * scale_row
    size = jnp.sum(err * err)
    good = size < 1e-8

    @pl.when(jnp.logical_not(good))
    def _():
        s_ref[...] = corr
        x_ref[...] = one

        def body(k, carry):
            row = s_ref[pl.ds(k, 1), :]
            rr, cc = iotas()
            ident = rr == cc
            lane = lax.broadcasted_iota(jnp.int32, (1, B), 1)
            pivot = jnp.sum(jnp.where(lane == k, row, 0.0), axis=1, keepdims=True)
            inv = lax.rsqrt(pivot)
            row = row * inv
            col = jnp.sum(jnp.where(ident, jnp.broadcast_to(row, (B, B)), 0.0), axis=1, keepdims=True)
            below = lax.broadcasted_iota(jnp.int32, (B, 1), 0) > k
            col = jnp.where(below, col, 0.0)
            xrow = x_ref[pl.ds(k, 1), :] * inv
            x_ref[pl.ds(k, 1), :] = xrow
            s_ref[...] = s_ref[...] - col * row
            x_ref[...] = x_ref[...] - col * xrow
            return carry

        lax.fori_loop(0, B, body, 0)
        out_ref[...] = x_ref[...] * scale_row


SMEM = pl.BlockSpec(memory_space=pltpu.SMEM)
VMEM = pl.BlockSpec(memory_space=pltpu.VMEM)


def shaped(*shape, dtype=F32):
    return jax.ShapeDtypeStruct(shape, dtype)


ANY = pl.BlockSpec(memory_space=pl.ANY)


def gram_kernel(panel):
    def body(p_ref, out_ref):
        p = p_ref[...]
        out_ref[...] = hdot(p, p, ((0,), (0,)))

    return pl.pallas_call(body, out_shape=shaped(B, B), compiler_params=params(), name="gram")(panel)


def product_kernel(panel, rinv, trailing, first_row, after):
    rows, cols = trailing.shape
    tile = 1024
    chunks = tile // B

    def body(first_ref, p_ref, r_ref, a_ref, *refs):
        v_ref, out_ref, vh_ref = refs[-3:]

        @pl.when(pl.program_id(0) == 0)
        def _():
            r, c = iotas((rows, B))
            v = dot3(p_ref[...], r_ref[...]) + jnp.where((r == c) & (first_ref[0] == 1), 1.0, 0.0)
            v_ref[...] = v
            vh_ref[:B], vh_ref[B:] = split(v.T)

        ah, al = split(a_ref[...])
        both = bdot(vh_ref[...], ah)
        z = both[:B] + (both[B:] + bdot(vh_ref[:B], al))
        for k in range(chunks):
            out_ref[k, 0] = z[:, k * B : (k + 1) * B]

    return pl.pallas_call(
        body,
        grid=(cols // tile,),
        out_shape=(shaped(rows, B), shaped(chunks, cols // tile, B, B)),
        in_specs=[
            SMEM,
            pl.BlockSpec((rows, B), lambda t: (0, 0)),
            pl.BlockSpec((B, B), lambda t: (0, 0)),
            pl.BlockSpec((rows, tile), lambda t: (0, t)),
        ]
        + [ANY] * len(after),
        out_specs=(
            pl.BlockSpec((rows, B), lambda t: (0, 0)),
            pl.BlockSpec((chunks, 1, B, B), lambda t: (0, t, 0, 0)),
        ),
        scratch_shapes=[pltpu.VMEM((2 * B, rows), BF16)],
        compiler_params=params(),
        cost_estimate=pl.CostEstimate(flops=6 * rows * cols * B, bytes_accessed=4 * rows * cols, transcendentals=0),
        name="product",
    )(first_row, panel, rinv, trailing, *after)


def factor_kernel(parts):
    def body(a_ref, b_ref, c_ref, d_ref, band_ref, rinv_ref, linv_ref, s_ref, x_ref):
        gram = (a_ref[...] + c_ref[...]) + (b_ref[...] + d_ref[...])
        inverse_factor(gram, linv_ref, s_ref, x_ref)
        linv = linv_ref[...]
        rinv_ref[...] = linv.T
        r, c = iotas()
        band_ref[...] = jnp.where(r <= c, -hdot(linv, gram), -0.0)

    square = shaped(B, B)
    return pl.pallas_call(
        body,
        out_shape=(square, square),
        scratch_shapes=[pltpu.VMEM((B, B), F32)] * 3,
        compiler_params=params(),
        name="factor",
    )(*parts)


def chunk_kernel(pieces, after):
    count = pieces.shape[0]

    def body(y_ref, after_ref, w_ref):
        total = [y_ref[k] for k in range(count)]
        while len(total) > 1:
            total = [l + r for l, r in zip(total[::2], total[1::2])]
        w_ref[...] = total[0].T

    return pl.pallas_call(
        body, out_shape=shaped(B, B), in_specs=[VMEM, ANY], compiler_params=params(), name="chunk"
    )(pieces, after)


def copies_kernel(w, v, count, after):
    def body(w_ref, v_ref, after_ref, copies_ref):
        for k in range(count):
            copies_ref[k, :, :B] = w_ref[...]
            copies_ref[k, :, B:] = v_ref[...]

    return pl.pallas_call(
        body, out_shape=shaped(count, B, 2 * B), in_specs=[VMEM, VMEM, ANY], compiler_params=pltpu.CompilerParams(vmem_limit_bytes=59 * 1024 * 1024), name="copies"
    )(w, v, after)


def small_kernel(right, after):
    rows = right.shape[0] * right.shape[1] * B

    def body(r_ref, after_ref, out_ref):
        both = r_ref[...].reshape(rows, 2 * B)
        out_ref[...] = dot3(both[:, B:], both[:, :B], ((0,), (0,)))

    return pl.pallas_call(
        body, out_shape=shaped(B, B), in_specs=[VMEM, ANY], compiler_params=params(), name="small"
    )(right, after)


def mixed_kernel(w_parts, coupling, place):
    part = w_parts[0].shape[0]

    def body(place_ref, t_ref, *refs):
        part_refs, out_ref = refs[:YN], refs[YN]
        for d in range(YN):
            y = lax.rem(place_ref[1] + (YN - d), YN)
            out_ref[pl.ds(pl.multiple_of(y * part, part), part), :] = dot3(part_refs[d][...], t_ref[...])

    return pl.pallas_call(
        body,
        out_shape=shaped(YN * part, B),
        in_specs=[SMEM] + [VMEM] * (YN + 1),
        compiler_params=params(),
        name="mixed",
    )(place, coupling, *w_parts)


def coupling_kernel(tops, rinv):
    def body(*refs):
        top_refs, (r_ref, out_ref, linv_ref, s_ref, x_ref) = refs[:4], refs[4:]
        top = (top_refs[0][...] + top_refs[1][...]) + (top_refs[2][...] + top_refs[3][...])
        m = eye() + hdot(top, r_ref[...]).T
        inverse_factor(hdot(m, m, ((0,), (0,))), linv_ref, s_ref, x_ref)
        linv = linv_ref[...]
        out_ref[...] = hdot(linv, hdot(linv, m, ((1,), (1,))), ((0,), (0,)))

    return pl.pallas_call(
        body,
        out_shape=shaped(B, B),
        scratch_shapes=[pltpu.VMEM((B, B), F32)] * 3,
        compiler_params=params(),
        name="coupling",
    )(*tops, rinv)


def turned_kernel(v, coupling):
    def body(v_ref, t_ref, h_ref, l_ref):
        h_ref[...], l_ref[...] = split(dot3(v_ref[...], t_ref[...], ((1,), (1,))))

    half = shaped(*v.shape, dtype=BF16)
    return pl.pallas_call(body, out_shape=(half, half), compiler_params=params(), name="turned")(v, coupling)


def update_kernel(trailing, right, v, turned, mixed, coupling, parts):
    rows, cols = trailing.shape
    tile = rows // 2
    halves = right.shape[1]
    wide = cols // halves

    def body(a_ref, right_ref, v_ref, th_ref, tl_ref, m_ref, t_ref, *refs):
        s_refs, (out_ref, small_ref, rh_ref, rl_ref) = refs[:YN], refs[YN:]

        @pl.when(pl.program_id(0) == 0)
        def _():
            t = t_ref[...]
            s = [ref[...] for ref in s_refs]
            small = hdot(hdot(t, (s[0] + s[2]) + (s[1] + s[3]), ((0,), (0,))), t)
            small_ref[...] = 0.5 * (small + small.T)
            for h in range(halves):
                at = slice(h * wide, (h + 1) * wide)
                rh_ref[at], rl_ref[at] = split(right_ref[:, h].reshape(wide, 2 * B))

        high, low = split(m_ref[...] - dot3(v_ref[...], small_ref[...]))
        high = jnp.concatenate([th_ref[...], high], axis=1)
        low = jnp.concatenate([tl_ref[...], low], axis=1)
        nt = ((1,), (1,))
        for k in range(0, cols, 512):
            at = slice(k, k + 512)
            rh, rl = rh_ref[at], rl_ref[at]
            out_ref[:, at] = a_ref[:, at] - (bdot(high, rh, nt) + (bdot(high, rl, nt) + bdot(low, rh, nt)))

    def whole(*shape):
        return pl.BlockSpec(shape, lambda t: (0,) * len(shape))

    def mine(width):
        return pl.BlockSpec((tile, width), lambda t: (t, 0))

    return pl.pallas_call(
        body,
        grid=(rows // tile,),
        out_shape=shaped(rows, cols),
        in_specs=[mine(cols), whole(*right.shape), mine(B), mine(B), mine(B), mine(B), whole(B, B)] + [whole(B, B)] * YN,
        out_specs=mine(cols),
        scratch_shapes=[pltpu.VMEM((B, B), F32)] + [pltpu.VMEM((cols, 2 * B), BF16)] * 2,
        compiler_params=params(),
        cost_estimate=pl.CostEstimate(flops=12 * rows * cols * B, bytes_accessed=8 * rows * cols, transcendentals=0),
        name="update",
    )(trailing, right, v, *turned, mixed, coupling, *parts)


def along_x(d):
    return [(z * XN + x, z * XN + (x + d) % XN) for z in range(ZN) for x in range(XN)]


def along_z(d):
    return [(z * XN + x, (z + d) % ZN * XN + x) for z in range(ZN) for x in range(XN)]


def along_y(d):
    return [(y * CN + c, (y + d) % YN * CN + c) for y in range(YN) for c in range(CN)]


def along_c(d):
    return [(y * CN + c, y * CN + (c + d) % CN) for y in range(YN) for c in range(CN)]


def four(value, axis, along):
    return [value] + [lax.ppermute(value, axis, along(d)) for d in (1, 2, 3)]


def add_four(parts):
    return (parts[0] + parts[2]) + (parts[1] + parts[3])


def to_all(copies, axis):
    return lax.all_to_all(copies, axis, split_axis=0, concat_axis=0, tiled=True)


def shards(panel, trailing):
    rows, cols = trailing.shape
    prow = lax.axis_size("prow")
    i, j = lax.axis_index("prow"), lax.axis_index("pcol")
    y, c, x = j // CN, j % CN, i % XN
    place = jnp.stack([i, y]).astype(jnp.int32)
    first_row = (i == 0).astype(jnp.int32).reshape(1)

    def device(z, x, y, c):
        return ((z * XN + x) * YN + y) * CN + c

    coords = [(z, x, y, c) for z in range(ZN) for x in range(XN) for y in range(YN) for c in range(CN)]
    swap = [(device(y, 2 * c + x % 2, z, x // 2), device(z, x, y, c)) for z, x, y, c in coords]

    top = jnp.where(i == 0, panel[:B], jnp.zeros_like(panel[:B]))
    parts = four(gram_kernel(panel), "prow", along_x)
    top = top + sum(lax.ppermute(top, "prow", [(0, k)]) for k in range(1, XN))
    parts = four(add_four(parts), "prow", along_z)
    tops = [top] + [lax.ppermute(top, "prow", [(k, z * XN + k) for k in range(XN)]) for z in range(1, ZN)]
    band, rinv = factor_kernel(parts)
    v, chunks = product_kernel(panel, rinv, trailing, first_row, tops)
    pieces = to_all(chunks.reshape(prow, B, B), "prow")

    v_chunk = lax.ppermute(lax.dynamic_slice_in_dim(v, j * B, B, 0), ("prow", "pcol"), swap)
    tops[0], _ = lax.optimization_barrier((tops[0], v))
    coupling = coupling_kernel(tops, rinv)
    turned = turned_kernel(v, coupling)

    w = chunk_kernel(pieces, turned[0])
    row_w = lax.ppermute(w, ("prow", "pcol"), swap)
    right = to_all(copies_kernel(w, v_chunk, prow, row_w), "prow").reshape(*chunks.shape[:3], 2 * B)

    other = lax.ppermute(row_w, "pcol", along_c(1))
    row_w = jnp.concatenate([jnp.where(c == 0, row_w, other), jnp.where(c == 0, other, row_w)])
    mixed = mixed_kernel(four(row_w, "pcol", along_y), coupling, place)

    part = small_kernel(right, mixed)
    part = part + lax.ppermute(part, "pcol", along_c(1))
    parts = four(part, "pcol", along_y)
    return update_kernel(trailing, right, v, turned, mixed, coupling, parts), band


def solution(mesh):
    placed = (P("prow", None), P("prow", "pcol"))
    return jax.shard_map(
        shards, mesh=mesh, in_specs=placed, out_specs=(P("prow", "pcol"), P()), check_vma=False
    )
```
